32 devices in a mesh: row: 4 (over y, x), col: 8 (over z, core).
Axes of the slice: x: 2, y: 2, z: 4, core: 2. Of those that a mesh axis runs over, the one named last changes fastest.
Arguments:
- diag_blocks: float32 [2, 512, 512], replicated, may hold values from -1 to 5, as said below
- pivot_flags: int32 [2, 512], replicated, may hold values 0 or 1
- panels: bfloat16 [2, 8192, 512], P(None, ('row', 'col')), may hold values from -3 to 3
- structure: int32 [2, 8192], P(None, ('row', 'col')), may hold values 0 or 1
- ancestor_inverse: bfloat16 [8192, 8192], P('row', 'col'), may hold values from -0.09375 to 0.09375
Outputs:
- inverse_panel: bfloat16 [2, 8192, 512], P(None, ('row', 'col'))
- inverse_diagonal: float32 [2, 512, 512], replicated
The draws below stay inside these ranges and needn't reach their ends.
Inputs may be any that keep to these rules, and one draw needn't show every extreme that they name: Each diag_blocks[k] is symmetric, and its off-diagonal part is small enough that every eigenvalue of each shifted block is at least 0.8, so every shifted block is positive definite.
All inputs are finite; a program needn't handle non-finite values. No bound on the sum of `structure` on one device may be relied on, other than what follows from the above.
Results may differ from the reference program's by a relative error of at most 0.0051.
Values may be sent and summed in bfloat16 or wider, within the bound.
A program may use at most 192 MiB of HBM per device.

```python
import math
import jax
import jax.numpy as jnp
from jax import lax

W = 512
NODES = 2
R = 8192
N_ROW = 4


def draw_diag_blocks(key, part):
    key_off, key_diag = jax.random.split(jax.random.fold_in(key, 11))
    spread_off = 0.6
    lower_end = 2.0
    upper_end = 4.0
    noise_term = jax.random.normal(key_off, (NODES, W, W), jnp.float32) * (spread_off / math.sqrt(W))
    symmetric = (noise_term + jnp.swapaxes(noise_term, 1, 2)) / math.sqrt(2.0)
    identity = jnp.eye(W, dtype=jnp.float32)
    symmetric = symmetric * (1.0 - identity)[None, :, :]
    diagonal = jax.random.uniform(key_diag, (NODES, W), jnp.float32, lower_end, upper_end)
    return symmetric + identity[None, :, :] * diagonal[:, None, :]


def touch_ends(entries, stream_key, low, high):
    dims = entries.shape
    spot = [jax.random.randint(jax.random.fold_in(stream_key, axis), (), 0, dims[axis]) for axis in range(len(dims))]
    entries = entries.at[tuple(spot)].set(low)
    longest = dims.index(max(dims))
    spot[longest] = (spot[longest] + 1) % dims[longest]
    return entries.at[tuple(spot)].set(high)


def raised(result, stream_key, source, target, parts, factor):
    owner, partner = [(jnp.arange(result.shape[position]) // (result.shape[position] // parts)).reshape([-1 if axis == position else 1 for axis in range(result.ndim)]) for position in (source, target)]
    chosen = jax.random.permutation(stream_key, parts)[partner]
    strong = (owner == chosen) | (owner == (partner + parts // 2) % parts)
    return jnp.where(strong, factor * result, result)


def shard_levels(stream_key, extent, pieces, smallest, top_value):
    factor_of = 1.0
    for dim, blocks in pieces:
        heights = jax.random.uniform(jax.random.fold_in(jax.random.fold_in(stream_key, 6), dim), (blocks,), jnp.float32, smallest / len(pieces), top_value / len(pieces))
        factor_of = factor_of * jnp.repeat(jnp.exp(heights), extent[dim] // blocks).reshape((-1,) + (1,) * (len(extent) - 1 - dim))
    return factor_of


def noise(rng, extent, scale, limit, shards=(), kind=jnp.bfloat16):
    loudness = shard_levels(rng, extent, shards, -0.22, 0.18) if shards else 1.0
    drawn = jax.random.normal(rng, extent, jnp.float32) * scale * loudness
    return jnp.minimum(jnp.maximum(drawn, -limit), limit).astype(kind)


def noise_with(key, extent, width, bound, pieces, heavy, held_as=jnp.bfloat16):
    values = width * jax.random.normal(key, extent, jnp.float32)
    if pieces:
        values = values * shard_levels(key, extent, pieces, -0.22, 0.18)
    return jnp.clip(raised(values, jax.random.fold_in(key, 3), *heavy), -bound, bound).astype(held_as)


def setup_inputs(seed: int = 0) -> dict:
    seeds = jax.random.split(jax.random.key(seed), 6)
    return {
        "diag_blocks": draw_diag_blocks(jax.random.fold_in(seeds[5], 71), 0),
        "pivot_flags": touch_ends((jax.random.randint(seeds[1], (NODES, W), 0, 4) < 1).astype(jnp.int32), jax.random.fold_in(seeds[1], 1), 0, 1),
        "panels": noise(seeds[2], (NODES, R, W), 0.5, 3.0, ((1, 32),)),
        "structure": touch_ends((jax.random.randint(seeds[3], (NODES, R), 0, 4) < 3).astype(jnp.int32), jax.random.fold_in(seeds[3], 1), 0, 1),
        "ancestor_inverse": noise_with(seeds[4], (R, R), R ** -0.5, 0.09375, ((0, 4), (1, 8)), (1, 0, 8, 2.0)),
    }


HIGHEST_PRECISION = lax.Precision.HIGHEST
PERTURBATION = 1.0

def factor_inverse(diagonal_block, flag_row):
    node_width = diagonal_block.shape[0]
    identity = jnp.eye(node_width, dtype=jnp.float32)
    shifted = diagonal_block + PERTURBATION * identity * flag_row.astype(jnp.float32)[None, :]
    factor_lower = jnp.linalg.cholesky(shifted)
    lower_inverse = jax.scipy.linalg.solve_triangular(factor_lower, identity, lower=True)
    return jnp.dot(lower_inverse.T, lower_inverse, precision=HIGHEST_PRECISION)

def normalize_panel(panel_rows, member_row, inverse):
    masked = panel_rows.astype(jnp.float32) * member_row.astype(jnp.float32)[:, None]
    return jnp.dot(masked, inverse, precision=HIGHEST_PRECISION).astype(jnp.bfloat16)

def reference(diag_blocks, pivot_flags, panels, structure, ancestor_inverse):
    matrix_order = ancestor_inverse.shape[0]
    tile_rows = matrix_order // N_ROW
    blocks = ancestor_inverse.reshape(N_ROW, tile_rows, matrix_order)
    panel_list = []
    diagonal_list = []
    for supernode in range(diag_blocks.shape[0]):
        inverse = factor_inverse(diag_blocks[supernode], pivot_flags[supernode])
        normed = normalize_panel(panels[supernode], structure[supernode], inverse)
        normed_wide = normed.astype(jnp.float32)

        def product(block_rows):
            return jnp.dot(block_rows.astype(jnp.float32), normed_wide, precision=HIGHEST_PRECISION)
        applied = lax.map(product, blocks).reshape(matrix_order, normed.shape[1])
        panel_list.append((-applied).astype(jnp.bfloat16))
        diagonal_list.append(inverse + jnp.dot(normed_wide.T, applied, precision=HIGHEST_PRECISION))
    return (jnp.stack(panel_list), jnp.stack(diagonal_list))
```

```python
import functools

import jax
import jax.numpy as jnp
from jax import lax
from jax.experimental import pallas as pl
from jax.experimental.pallas import tpu as pltpu
from jax.sharding import PartitionSpec as P

MESH = pl.DeviceIdType.MESH
PERTURBATION = 1.0
EIG_LOW = 0.8
STEPS = 9
BF = jnp.bfloat16
F32 = jnp.float32


def split(x):
    hi = x.astype(BF)
    return hi, (x - hi.astype(F32)).astype(BF)


def dot3(a, b):
    ah, al = a
    bh, bl = b
    d = functools.partial(jnp.dot, preferred_element_type=F32)
    return d(ah, bh) + (d(ah, bl) + d(al, bh))


def eye(width):
    r = lax.broadcasted_iota(jnp.int32, (width, width), 0)
    c = lax.broadcasted_iota(jnp.int32, (width, width), 1)
    return (r == c).astype(F32)


def spread_kernel(n_row, n_col, panel, diag, flags, pc, inv, shifted, ah, al, send, recv, own):
    nodes, width = diag.shape[0], diag.shape[1]
    r, c = lax.axis_index("row"), lax.axis_index("col")
    me = r * n_col + c
    target_col = me // n_row
    slot = lax.rem(me, n_row)

    barrier = pltpu.get_barrier_semaphore()
    for j in range(n_row):
        q = c * n_row + j

        @pl.when(q != me)
        def _(q=q):
            pl.semaphore_signal(barrier, inc=1, device_id=(q // n_col, lax.rem(q, n_col)), device_id_type=MESH)

    pl.semaphore_wait(barrier, n_row - (target_col == c).astype(jnp.int32))

    def copy(dest_row, dest_slot, sem_slot):
        return pltpu.make_async_remote_copy(
            src_ref=panel,
            dst_ref=pc.at[dest_slot],
            send_sem=send.at[sem_slot],
            recv_sem=recv.at[dest_slot],
            device_id=(dest_row, target_col),
            device_id_type=MESH,
        )

    local = pltpu.make_async_copy(panel, pc.at[slot], own)
    for off in range(n_row):
        dest = lax.rem(r + off, n_row)
        is_me = jnp.logical_and(dest == r, target_col == c)

        @pl.when(is_me)
        def _():
            local.start()

        @pl.when(jnp.logical_not(is_me))
        def _(dest=dest, off=off):
            copy(dest, slot, off).start()

    low = []
    for k in range(nodes):
        a = diag[k] + PERTURBATION * eye(width) * flags[k].astype(F32)
        shifted[k] = a
        ah[k], al[k] = split(a)
        top = jnp.max(jnp.sum(jnp.abs(a), axis=0, keepdims=True), axis=1, keepdims=True)
        top = jnp.broadcast_to(top, (1, width))
        x0 = 2.0 / (EIG_LOW + top)
        low0 = EIG_LOW * x0
        grown = low0 * (2.0 - low0)
        scale = 2.0 / (1.0 + grown)
        inv[k] = (scale * x0) * (2.0 * eye(width) - x0 * a)
        low.append(scale * grown)

    def body(_, low):
        out = []
        for k in range(nodes):
            x = split(inv[k])
            rest = 2.0 * eye(width) - dot3((ah[k], al[k]), x)
            grown = low[k] * (2.0 - low[k])
            scale = 2.0 / (1.0 + grown)
            inv[k] = scale * dot3(x, split(rest))
            out.append(scale * grown)
        return tuple(out)

    lax.fori_loop(0, STEPS - 2, body, tuple(low))
    for k in range(nodes):
        x = inv[k]
        rest = eye(width) - jnp.dot(
            shifted[k], x, precision=lax.Precision.HIGHEST, preferred_element_type=F32
        )
        inv[k] = x + dot3(split(x), split(rest))

    for off in range(n_row):
        dest = lax.rem(r + off, n_row)
        is_me = jnp.logical_and(dest == r, target_col == c)

        @pl.when(is_me)
        def _():
            local.wait()

        @pl.when(jnp.logical_not(is_me))
        def _(dest=dest, off=off):
            copy(dest, slot, off).wait_send()

    for j in range(n_row):
        q = c * n_row + j

        @pl.when(q != me)
        def _(j=j):
            copy(0, j, 0).wait_recv()


def spread(n_row, n_col, panel, diag, flags):
    nodes, width = diag.shape[0], diag.shape[1]
    vm = pl.BlockSpec(memory_space=pltpu.VMEM)
    return pl.pallas_call(
        functools.partial(spread_kernel, n_row, n_col),
        out_shape=(
            jax.ShapeDtypeStruct((n_row,) + panel.shape, BF),
            jax.ShapeDtypeStruct(diag.shape, F32),
        ),
        in_specs=[vm] * 3,
        out_specs=(vm, vm),
        scratch_shapes=[
            pltpu.VMEM(diag.shape, F32),
            pltpu.VMEM(diag.shape, BF),
            pltpu.VMEM(diag.shape, BF),
            pltpu.SemaphoreType.DMA((n_row,)),
            pltpu.SemaphoreType.DMA((n_row,)),
            pltpu.SemaphoreType.DMA,
        ],
        compiler_params=pltpu.CompilerParams(
            collective_id=0, has_side_effects=True, vmem_limit_bytes=48 * 2**20
        ),
        name="spread_panels_and_invert",
    )(panel, diag, flags)


def reduce_kernel(
    n_row, n_col, part, normed, inv, panel_out, diag_out,
    pair_in, line_out, line_in, dpart, dpair, drow, dline, piece,
    pair_s, pair_r, line_s, line_r, da_s, da_r, db_s, db_r, dc_s, dc_r,
    gc_s, gc_r, gb_s, gb_r, ga_s, ga_r,
):
    nz = n_col // 2
    nodes, width = inv.shape[0], inv.shape[1]
    r, c = lax.axis_index("row"), lax.axis_index("col")
    z, core = c // 2, lax.rem(c, 2)
    other = 1 - core
    pair = (r, z * 2 + other)

    def line(off):
        zz = lax.rem(z + off, nz)
        return zz, (r, zz * 2 + core)

    def across(off):
        rr = lax.rem(r + off, n_row)
        return rr, (rr, c)

    def rc(src, dst, s, q, dev):
        return pltpu.make_async_remote_copy(
            src_ref=src, dst_ref=dst, send_sem=s, recv_sem=q, device_id=dev, device_id_type=MESH
        )

    barrier = pltpu.get_barrier_semaphore()
    pl.semaphore_signal(barrier, inc=1, device_id=pair, device_id_type=MESH)
    for off in range(1, nz):
        pl.semaphore_signal(barrier, inc=1, device_id=line(off)[1], device_id_type=MESH)
    for off in range(1, n_row):
        pl.semaphore_signal(barrier, inc=1, device_id=across(off)[1], device_id_type=MESH)
    pl.semaphore_wait(barrier, 1 + (nz - 1) + (n_row - 1))

    order = list(range(1, nz)) + [0]
    pair_copies = {}
    for off in order:
        zz, _ = line(off)
        pair_copies[off] = rc(
            part.at[zz * 2 + other], pair_in.at[off], pair_s.at[off], pair_r.at[off], pair
        )
        pair_copies[off].start()
    line_copies = {}
    for off in range(1, nz):
        zz, dev = line(off)
        pair_copies[off].wait_recv()
        line_out[off - 1] = (
            part[zz * 2 + core].astype(F32) + pair_in[off].astype(F32)
        ).astype(BF)
        line_copies[off] = rc(
            line_out.at[off - 1], line_in.at[off - 1], line_s.at[off - 1], line_r.at[off - 1], dev
        )
        line_copies[off].start()
    pair_copies[0].wait_recv()
    for off in range(1, nz):
        line_copies[off].wait_recv()

    for k in range(nodes):
        cols = pl.ds(k * width, width)
        applied = part[c, :, cols].astype(F32) + pair_in[0, :, cols].astype(F32)
        for off in range(1, nz):
            applied = applied + line_in[off - 1, :, cols].astype(F32)
        panel_out[k] = (-applied).astype(BF)
        hi, lo = split(applied)
        left = normed[:, cols]
        dims = (((0,), (0,)), ((), ()))
        dpart[k] = lax.dot_general(left, hi, dims, preferred_element_type=F32) + lax.dot_general(
            left, lo, dims, preferred_element_type=F32
        )

    half = nodes // 2
    first = core * half
    hold = pl.ds(first, half)
    copy = rc(dpart.at[pl.ds(other * half, half)], dpair, da_s.at[0], da_r.at[0], pair)
    copy.start()
    copy.wait_recv()
    dpart[hold] = dpart[hold] + dpair[...]
    copies = [copy]

    rows_b = width // n_row
    stage = []
    for off in range(1, n_row):
        rr, dev = across(off)
        cp = rc(
            dpart.at[hold, pl.ds(rr * rows_b, rows_b)],
            drow.at[off - 1], db_s.at[off - 1], db_r.at[off - 1], dev,
        )
        cp.start()
        stage.append(cp)
    start_b = pl.multiple_of(r * rows_b, rows_b)
    for cp in stage:
        cp.wait_recv()
    total = dpart[hold, pl.ds(start_b, rows_b)]
    for off in range(1, n_row):
        total = total + drow[off - 1]
    piece[...] = total
    copies += stage

    rows_c = rows_b // nz
    stage = []
    for off in range(1, nz):
        zz, dev = line(off)
        cp = rc(
            piece.at[:, pl.ds(zz * rows_c, rows_c)],
            dline.at[off - 1], dc_s.at[off - 1], dc_r.at[off - 1], dev,
        )
        cp.start()
        stage.append(cp)
    start_c = pl.multiple_of(z * rows_c, rows_c)
    for cp in stage:
        cp.wait_recv()
    total = piece[:, pl.ds(start_c, rows_c)]
    for off in range(1, nz):
        total = total + dline[off - 1]
    mine = pl.multiple_of(start_b + start_c, rows_c)
    diag_out[hold, pl.ds(mine, rows_c)] = total + inv[hold, pl.ds(mine, rows_c)]
    copies += stage

    stage = []
    for off in range(1, nz):
        _, dev = line(off)
        at = diag_out.at[hold, pl.ds(mine, rows_c)]
        cp = rc(at, at, gc_s.at[off - 1], gc_r.at[off - 1], dev)
        cp.start()
        stage.append(cp)
    for cp in stage:
        cp.wait_recv()
    copies += stage
    stage = []
    for off in range(1, n_row):
        _, dev = across(off)
        at = diag_out.at[hold, pl.ds(start_b, rows_b)]
        cp = rc(at, at, gb_s.at[off - 1], gb_r.at[off - 1], dev)
        cp.start()
        stage.append(cp)
    for cp in stage:
        cp.wait_recv()
    copies += stage
    at = diag_out.at[hold]
    cp = rc(at, at, ga_s.at[0], ga_r.at[0], pair)
    cp.start()
    cp.wait_recv()
    copies.append(cp)
    for off in order:
        pair_copies[off].wait_send()
    for off in range(1, nz):
        line_copies[off].wait_send()
    for cp in copies:
        cp.wait_send()


def reduce(n_row, n_col, part, normed, inv):
    nz = n_col // 2
    nodes, width = inv.shape[0], inv.shape[1]
    rows = normed.shape[0]
    half = nodes // 2
    rows_b = width // n_row
    rows_c = rows_b // nz
    vm = pl.BlockSpec(memory_space=pltpu.VMEM)
    dma = pltpu.SemaphoreType.DMA
    return pl.pallas_call(
        functools.partial(reduce_kernel, n_row, n_col),
        out_shape=(
            jax.ShapeDtypeStruct((nodes, rows, width), BF),
            jax.ShapeDtypeStruct(inv.shape, F32),
        ),
        in_specs=[vm] * 3,
        out_specs=(vm, vm),
        scratch_shapes=[
            pltpu.VMEM((nz, rows, nodes * width), BF),
            pltpu.VMEM((nz - 1, rows, nodes * width), BF),
            pltpu.VMEM((nz - 1, rows, nodes * width), BF),
            pltpu.VMEM(inv.shape, F32),
            pltpu.VMEM((half, width, width), F32),
            pltpu.VMEM((n_row - 1, half, rows_b, width), F32),
            pltpu.VMEM((nz - 1, half, rows_c, width), F32),
            pltpu.VMEM((half, rows_b, width), F32),
            dma((nz,)), dma((nz,)), dma((nz - 1,)), dma((nz - 1,)),
            dma((1,)), dma((1,)), dma((n_row - 1,)), dma((n_row - 1,)),
            dma((nz - 1,)), dma((nz - 1,)), dma((nz - 1,)), dma((nz - 1,)),
            dma((n_row - 1,)), dma((n_row - 1,)), dma((1,)), dma((1,)),
        ],
        compiler_params=pltpu.CompilerParams(
            collective_id=1, has_side_effects=True, vmem_limit_bytes=48 * 2**20
        ),
        name="sum_products_and_diagonals",
    )(part, normed, inv)


def normalize(rows, inv):
    hi, lo = split(inv)
    dims = (((2,), (1,)), ((0,), (0,)))
    d = functools.partial(lax.dot_general, dimension_numbers=dims, preferred_element_type=F32)
    return (d(rows, hi) + d(rows, lo)).astype(BF)


def local(n_row, n_col, diag_blocks, pivot_flags, panels, structure, ancestor_inverse):
    nodes, rows, width = panels.shape
    masked = panels * structure.astype(BF)[:, :, None]
    column, inv = spread(n_row, n_col, masked, diag_blocks, pivot_flags[:, None, :])
    column = column.transpose(1, 0, 2, 3).reshape(nodes, n_row * rows, width)
    block = normalize(column, inv).transpose(1, 0, 2).reshape(n_row * rows, nodes * width)
    own = normalize(masked, inv).transpose(1, 0, 2).reshape(rows, nodes * width)
    part = jnp.dot(ancestor_inverse, block, preferred_element_type=F32).astype(BF)
    part = part.reshape(n_col, rows, nodes * width)
    return reduce(n_row, n_col, part, own, inv)


def solution(mesh):
    in_specs = (P(), P(), P(None, ("row", "col"), None), P(None, ("row", "col")), P("row", "col"))
    out_specs = (P(None, ("row", "col"), None), P())
    body = functools.partial(local, mesh.shape["row"], mesh.shape["col"])
    return jax.shard_map(body, mesh=mesh, in_specs=in_specs, out_specs=out_specs, check_vma=False)
```

```python
import functools

import jax
import jax.numpy as jnp
from jax import lax
from jax.experimental import pallas as pl
from jax.experimental.pallas import tpu as pltpu
from jax.sharding import PartitionSpec as P

MESH = pl.DeviceIdType.MESH
PERTURBATION = 1.0
EIG_LOW = 0.8
STEPS = 9
BF = jnp.bfloat16
F32 = jnp.float32


def split(x):
    hi = x.astype(BF)
    return hi, (x - hi.astype(F32)).astype(BF)


def dot3(a, b):
    ah, al = a
    bh, bl = b
    d = functools.partial(jnp.dot, preferred_element_type=F32)
    return d(ah, bh) + (d(ah, bl) + d(al, bh))


def eye(width):
    r = lax.broadcasted_iota(jnp.int32, (width, width), 0)
    c = lax.broadcasted_iota(jnp.int32, (width, width), 1)
    return (r == c).astype(F32)


def spread_kernel(
    n_row, n_col, panel, diag, flags, pc, inv, held, shifted, ah, al,
    s1, r1, s2, r2, s3, r3, sx, rx,
):
    nodes, width = diag.shape[0], diag.shape[1]
    ratio = n_col // n_row
    half = nodes // 2
    r, c = lax.axis_index("row"), lax.axis_index("col")
    core = lax.rem(c, 2)
    pair = (r, c + 1 - 2 * core)
    slot = lax.rem(c, n_row)
    count = panel.shape[1] // n_row

    def rows(i):
        return pl.ds(pl.multiple_of(i * count, count), count)

    def goal(row):
        return row * ratio + c // n_row

    def across(off):
        return lax.rem(r + off, n_row)

    def rc(src, dst, s, q, dev):
        return pltpu.make_async_remote_copy(
            src_ref=src, dst_ref=dst, send_sem=s, recv_sem=q, device_id=dev, device_id_type=MESH
        )

    barrier = pltpu.get_barrier_semaphore()
    pl.semaphore_signal(barrier, inc=1, device_id=pair, device_id_type=MESH)
    expect = n_row
    for off in range(1, n_row):
        pl.semaphore_signal(barrier, inc=1, device_id=(across(off), c), device_id_type=MESH)
    for j in range(n_row):
        sender = lax.rem(n_row * c + j, n_col)

        @pl.when(sender != c)
        def _(sender=sender):
            pl.semaphore_signal(barrier, inc=1, device_id=(r, sender), device_id_type=MESH)

        expect = expect + (goal(j) != c).astype(jnp.int32)
    pl.semaphore_wait(barrier, expect)

    first = []
    for off in range(1, n_row):
        to = across(off)
        cp = rc(panel.at[:, rows(to)], held.at[r], s1.at[off - 1], r1.at[off - 1], (to, c))
        cp.start()
        first.append(cp)
    held[r] = panel[:, rows(r)]

    def second(j):
        return rc(held.at[j], pc.at[slot, :, rows(r)], s2.at[j], r2.at[slot], (r, goal(j)))

    def forward():
        for cp in first:
            cp.wait_recv()
        for j in range(n_row):

            @pl.when(goal(j) != c)
            def _(j=j):
                second(j).start()

            @pl.when(goal(j) == c)
            def _(j=j):
                pc[slot, :, rows(r)] = held[j]

    third = []

    def gather():
        for j in range(n_row):
            sender = lax.rem(n_row * c + j, n_col)

            @pl.when(sender != c)
            def _(j=j):
                at = pc.at[j, :, rows(r)]
                rc(held.at[0], at, s2.at[0], r2.at[j], pair).wait_recv()

            at = pc.at[j, :, rows(r)]
            for off in range(1, n_row):
                cp = rc(at, at, s3.at[off - 1, j], r3.at[off - 1, j], (across(off), c))
                cp.start()
                third.append(cp)

    low = []
    for i in range(half):
        k = core * half + i
        a = diag[k] + PERTURBATION * eye(width) * flags[k].astype(F32)
        shifted[i] = a
        ah[i], al[i] = split(a)
        top = jnp.max(jnp.sum(jnp.abs(a), axis=0, keepdims=True), axis=1, keepdims=True)
        top = jnp.broadcast_to(top, (1, width))
        x0 = 2.0 / (EIG_LOW + top)
        low0 = EIG_LOW * x0
        grown = low0 * (2.0 - low0)
        scale = 2.0 / (1.0 + grown)
        inv[k] = (scale * x0) * (2.0 * eye(width) - x0 * a)
        low.append(scale * grown)

    def body(_, low):
        out = []
        for i in range(half):
            k = core * half + i
            x = split(inv[k])
            rest = 2.0 * eye(width) - dot3((ah[i], al[i]), x)
            grown = low[i] * (2.0 - low[i])
            scale = 2.0 / (1.0 + grown)
            inv[k] = scale * dot3(x, split(rest))
            out.append(scale * grown)
        return tuple(out)

    low = lax.fori_loop(0, 2, body, tuple(low))
    forward()
    low = lax.fori_loop(0, 3, body, low)
    gather()
    lax.fori_loop(0, STEPS - 7, body, low)
    for i in range(half):
        k = core * half + i
        x = inv[k]
        rest = eye(width) - jnp.dot(
            shifted[i], x, precision=lax.Precision.HIGHEST, preferred_element_type=F32
        )
        inv[k] = x + dot3(split(x), split(rest))
    at = inv.at[pl.ds(core * half, half)]
    swap = rc(at, at, sx.at[0], rx.at[0], pair)
    swap.start()
    swap.wait_recv()
    for cp in third:
        cp.wait_recv()
    swap.wait_send()
    for cp in first + third:
        cp.wait_send()
    for j in range(n_row):

        @pl.when(goal(j) != c)
        def _(j=j):
            second(j).wait_send()


def spread(n_row, n_col, panel, diag, flags):
    nodes, width = diag.shape[0], diag.shape[1]
    vm = pl.BlockSpec(memory_space=pltpu.VMEM)
    dma = pltpu.SemaphoreType.DMA
    some = (nodes // 2,) + diag.shape[1:]
    return pl.pallas_call(
        functools.partial(spread_kernel, n_row, n_col),
        out_shape=(
            jax.ShapeDtypeStruct((n_row,) + panel.shape, BF),
            jax.ShapeDtypeStruct(diag.shape, F32),
        ),
        in_specs=[vm] * 3,
        out_specs=(vm, vm),
        scratch_shapes=[
            pltpu.VMEM((n_row, nodes, panel.shape[1] // n_row, width), BF),
            pltpu.VMEM(some, F32),
            pltpu.VMEM(some, BF),
            pltpu.VMEM(some, BF),
            dma((n_row - 1,)), dma((n_row - 1,)),
            dma((n_row,)), dma((n_row,)),
            dma((n_row - 1, n_row)), dma((n_row - 1, n_row)),
            dma((1,)), dma((1,)),
        ],
        compiler_params=pltpu.CompilerParams(
            collective_id=0, has_side_effects=True, vmem_limit_bytes=48 * 2**20
        ),
        name="spread_panels_and_invert",
    )(panel, diag, flags)


def reduce_kernel(
    n_row, n_col, part, normed, inv, panel_out, diag_out,
    pair_in, line_out, line_in, dpart, dpair, drow, dline, piece,
    pair_s, pair_r, line_s, line_r, da_s, da_r, db_s, db_r, dc_s, dc_r,
    gc_s, gc_r, gb_s, gb_r, ga_s, ga_r,
):
    nz = n_col // 2
    nodes, width = inv.shape[0], inv.shape[1]
    r, c = lax.axis_index("row"), lax.axis_index("col")
    z, core = c // 2, lax.rem(c, 2)
    other = 1 - core
    pair = (r, z * 2 + other)

    def line(off):
        zz = lax.rem(z + off, nz)
        return zz, (r, zz * 2 + core)

    def across(off):
        rr = lax.rem(r + off, n_row)
        return rr, (rr, c)

    def rc(src, dst, s, q, dev):
        return pltpu.make_async_remote_copy(
            src_ref=src, dst_ref=dst, send_sem=s, recv_sem=q, device_id=dev, device_id_type=MESH
        )

    barrier = pltpu.get_barrier_semaphore()
    pl.semaphore_signal(barrier, inc=1, device_id=pair, device_id_type=MESH)
    for off in range(1, nz):
        pl.semaphore_signal(barrier, inc=1, device_id=line(off)[1], device_id_type=MESH)
    for off in range(1, n_row):
        pl.semaphore_signal(barrier, inc=1, device_id=across(off)[1], device_id_type=MESH)
    pl.semaphore_wait(barrier, 1 + (nz - 1) + (n_row - 1))

    order = list(range(1, nz)) + [0]
    pair_copies = {}
    for off in order:
        zz, _ = line(off)
        pair_copies[off] = rc(
            part.at[zz * 2 + other], pair_in.at[off], pair_s.at[off], pair_r.at[off], pair
        )
        pair_copies[off].start()
    line_copies = {}
    for off in range(1, nz):
        zz, dev = line(off)
        pair_copies[off].wait_recv()
        line_out[off - 1] = (
            part[zz * 2 + core].astype(F32) + pair_in[off].astype(F32)
        ).astype(BF)
        line_copies[off] = rc(
            line_out.at[off - 1], line_in.at[off - 1], line_s.at[off - 1], line_r.at[off - 1], dev
        )
        line_copies[off].start()
    pair_copies[0].wait_recv()
    for off in range(1, nz):
        line_copies[off].wait_recv()

    for k in range(nodes):
        cols = pl.ds(k * width, width)
        applied = part[c, :, cols].astype(F32) + pair_in[0, :, cols].astype(F32)
        for off in range(1, nz):
            applied = applied + line_in[off - 1, :, cols].astype(F32)
        panel_out[k] = (-applied).astype(BF)
        hi, lo = split(applied)
        left = normed[:, cols]
        dims = (((0,), (0,)), ((), ()))
        dpart[k] = lax.dot_general(left, hi, dims, preferred_element_type=F32) + lax.dot_general(
            left, lo, dims, preferred_element_type=F32
        )

    half = nodes // 2
    first = core * half
    hold = pl.ds(first, half)
    copy = rc(dpart.at[pl.ds(other * half, half)], dpair, da_s.at[0], da_r.at[0], pair)
    copy.start()
    copy.wait_recv()
    dpart[hold] = dpart[hold] + dpair[...]
    copies = [copy]

    rows_b = width // n_row
    stage = []
    for off in range(1, n_row):
        rr, dev = across(off)
        cp = rc(
            dpart.at[hold, pl.ds(rr * rows_b, rows_b)],
            drow.at[off - 1], db_s.at[off - 1], db_r.at[off - 1], dev,
        )
        cp.start()
        stage.append(cp)
    start_b = pl.multiple_of(r * rows_b, rows_b)
    for cp in stage:
        cp.wait_recv()
    total = dpart[hold, pl.ds(start_b, rows_b)]
    for off in range(1, n_row):
        total = total + drow[off - 1]
    piece[...] = total
    copies += stage

    rows_c = rows_b // nz
    stage = []
    for off in range(1, nz):
        zz, dev = line(off)
        cp = rc(
            piece.at[:, pl.ds(zz * rows_c, rows_c)],
            dline.at[off - 1], dc_s.at[off - 1], dc_r.at[off - 1], dev,
        )
        cp.start()
        stage.append(cp)
    start_c = pl.multiple_of(z * rows_c, rows_c)
    for cp in stage:
        cp.wait_recv()
    total = piece[:, pl.ds(start_c, rows_c)]
    for off in range(1, nz):
        total = total + dline[off - 1]
    mine = pl.multiple_of(start_b + start_c, rows_c)
    diag_out[hold, pl.ds(mine, rows_c)] = total + inv[hold, pl.ds(mine, rows_c)]
    copies += stage

    stage = []
    for off in range(1, nz):
        _, dev = line(off)
        at = diag_out.at[hold, pl.ds(mine, rows_c)]
        cp = rc(at, at, gc_s.at[off - 1], gc_r.at[off - 1], dev)
        cp.start()
        stage.append(cp)
    for cp in stage:
        cp.wait_recv()
    copies += stage
    stage = []
    for off in range(1, n_row):
        _, dev = across(off)
        at = diag_out.at[hold, pl.ds(start_b, rows_b)]
        cp = rc(at, at, gb_s.at[off - 1], gb_r.at[off - 1], dev)
        cp.start()
        stage.append(cp)
    for cp in stage:
        cp.wait_recv()
    copies += stage
    at = diag_out.at[hold]
    cp = rc(at, at, ga_s.at[0], ga_r.at[0], pair)
    cp.start()
    cp.wait_recv()
    copies.append(cp)
    for off in order:
        pair_copies[off].wait_send()
    for off in range(1, nz):
        line_copies[off].wait_send()
    for cp in copies:
        cp.wait_send()


def reduce(n_row, n_col, part, normed, inv):
    nz = n_col // 2
    nodes, width = inv.shape[0], inv.shape[1]
    rows = normed.shape[0]
    half = nodes // 2
    rows_b = width // n_row
    rows_c = rows_b // nz
    vm = pl.BlockSpec(memory_space=pltpu.VMEM)
    dma = pltpu.SemaphoreType.DMA
    return pl.pallas_call(
        functools.partial(reduce_kernel, n_row, n_col),
        out_shape=(
            jax.ShapeDtypeStruct((nodes, rows, width), BF),
            jax.ShapeDtypeStruct(inv.shape, F32),
        ),
        in_specs=[vm] * 3,
        out_specs=(vm, vm),
        scratch_shapes=[
            pltpu.VMEM((nz, rows, nodes * width), BF),
            pltpu.VMEM((nz - 1, rows, nodes * width), BF),
            pltpu.VMEM((nz - 1, rows, nodes * width), BF),
            pltpu.VMEM(inv.shape, F32),
            pltpu.VMEM((half, width, width), F32),
            pltpu.VMEM((n_row - 1, half, rows_b, width), F32),
            pltpu.VMEM((nz - 1, half, rows_c, width), F32),
            pltpu.VMEM((half, rows_b, width), F32),
            dma((nz,)), dma((nz,)), dma((nz - 1,)), dma((nz - 1,)),
            dma((1,)), dma((1,)), dma((n_row - 1,)), dma((n_row - 1,)),
            dma((nz - 1,)), dma((nz - 1,)), dma((nz - 1,)), dma((nz - 1,)),
            dma((n_row - 1,)), dma((n_row - 1,)), dma((1,)), dma((1,)),
        ],
        compiler_params=pltpu.CompilerParams(
            collective_id=1, has_side_effects=True, vmem_limit_bytes=48 * 2**20
        ),
        name="sum_products_and_diagonals",
    )(part, normed, inv)


def normalize(rows, inv):
    hi, lo = split(inv)
    dims = (((2,), (1,)), ((0,), (0,)))
    d = functools.partial(lax.dot_general, dimension_numbers=dims, preferred_element_type=F32)
    return (d(rows, hi) + d(rows, lo)).astype(BF)


def local(n_row, n_col, diag_blocks, pivot_flags, panels, structure, ancestor_inverse):
    nodes, rows, width = panels.shape
    masked = panels * structure.astype(BF)[:, :, None]
    column, inv = spread(n_row, n_col, masked, diag_blocks, pivot_flags[:, None, :])
    column = column.transpose(1, 0, 2, 3).reshape(nodes, n_row * rows, width)
    block = normalize(column, inv).transpose(1, 0, 2).reshape(n_row * rows, nodes * width)
    own = normalize(masked, inv).transpose(1, 0, 2).reshape(rows, nodes * width)
    part = jnp.dot(ancestor_inverse, block, preferred_element_type=F32).astype(BF)
    part = part.reshape(n_col, rows, nodes * width)
    return reduce(n_row, n_col, part, own, inv)


def solution(mesh):
    in_specs = (P(), P(), P(None, ("row", "col"), None), P(None, ("row", "col")), P("row", "col"))
    out_specs = (P(None, ("row", "col"), None), P())
    body = functools.partial(local, mesh.shape["row"], mesh.shape["col"])
    return jax.shard_map(body, mesh=mesh, in_specs=in_specs, out_specs=out_specs, check_vma=False)
```

```python
import functools

import jax
import jax.numpy as jnp
from jax import lax
from jax.experimental import pallas as pl
from jax.experimental.pallas import tpu as pltpu
from jax.sharding import PartitionSpec as P

MESH = pl.DeviceIdType.MESH
PERTURBATION = 1.0
EIG_LOW = 0.8
STEPS = 9
BF = jnp.bfloat16
F32 = jnp.float32


def split(x):
    hi = x.astype(BF)
    return hi, (x - hi.astype(F32)).astype(BF)


def dot3(a, b):
    ah, al = a
    bh, bl = b
    d = functools.partial(jnp.dot, preferred_element_type=F32)
    return d(ah, bh) + (d(ah, bl) + d(al, bh))


def eye(width):
    r = lax.broadcasted_iota(jnp.int32, (width, width), 0)
    c = lax.broadcasted_iota(jnp.int32, (width, width), 1)
    return (r == c).astype(F32)


def spread_kernel(
    n_row, n_col, panel, diag, flags, pc, inv, held, shifted, ah, al,
    s1, r1, s2, r2, s3, r3, sx, rx,
):
    nodes, width = diag.shape[0], diag.shape[1]
    ratio = n_col // n_row
    half = nodes // 2
    r, c = lax.axis_index("row"), lax.axis_index("col")
    core = lax.rem(c, 2)
    pair = (r, c + 1 - 2 * core)
    slot = lax.rem(c, n_row)
    count = panel.shape[1] // n_row

    def rows(i):
        return pl.ds(pl.multiple_of(i * count, count), count)

    def goal(row):
        return row * ratio + c // n_row

    def across(off):
        return lax.rem(r + off, n_row)

    def rc(src, dst, s, q, dev):
        return pltpu.make_async_remote_copy(
            src_ref=src, dst_ref=dst, send_sem=s, recv_sem=q, device_id=dev, device_id_type=MESH
        )

    barrier = pltpu.get_barrier_semaphore()
    pl.semaphore_signal(barrier, inc=1, device_id=pair, device_id_type=MESH)
    expect = n_row
    for off in range(1, n_row):
        pl.semaphore_signal(barrier, inc=1, device_id=(across(off), c), device_id_type=MESH)
    for j in range(n_row):
        sender = lax.rem(n_row * c + j, n_col)

        @pl.when(sender != c)
        def _(sender=sender):
            pl.semaphore_signal(barrier, inc=1, device_id=(r, sender), device_id_type=MESH)

        expect = expect + (goal(j) != c).astype(jnp.int32)
    pl.semaphore_wait(barrier, expect)

    first = []
    for off in range(1, n_row):
        to = across(off)
        cp = rc(panel.at[:, rows(to)], held.at[r], s1.at[off - 1], r1.at[off - 1], (to, c))
        cp.start()
        first.append(cp)
    held[r] = panel[:, rows(r)]

    def second(j):
        return rc(held.at[j], pc.at[slot, :, rows(r)], s2.at[j], r2.at[slot], (r, goal(j)))

    def forward():
        for cp in first:
            cp.wait_recv()
        for j in range(n_row):

            @pl.when(goal(j) != c)
            def _(j=j):
                second(j).start()

            @pl.when(goal(j) == c)
            def _(j=j):
                pc[slot, :, rows(r)] = held[j]

    third = []

    def gather():
        for j in range(n_row):
            sender = lax.rem(n_row * c + j, n_col)

            @pl.when(sender != c)
            def _(j=j):
                at = pc.at[j, :, rows(r)]
                rc(held.at[0], at, s2.at[0], r2.at[j], pair).wait_recv()

            at = pc.at[j, :, rows(r)]
            for off in range(1, n_row):
                cp = rc(at, at, s3.at[off - 1, j], r3.at[off - 1, j], (across(off), c))
                cp.start()
                third.append(cp)

    low = []
    for i in range(half):
        k = core * half + i
        a = diag[k] + PERTURBATION * eye(width) * flags[k].astype(F32)
        shifted[i] = a
        ah[i], al[i] = split(a)
        top = jnp.max(jnp.sum(jnp.abs(a), axis=0, keepdims=True), axis=1, keepdims=True)
        top = jnp.broadcast_to(top, (1, width))
        x0 = 2.0 / (EIG_LOW + top)
        low0 = EIG_LOW * x0
        grown = low0 * (2.0 - low0)
        scale = 2.0 / (1.0 + grown)
        inv[k] = (scale * x0) * (2.0 * eye(width) - x0 * a)
        low.append(scale * grown)

    def body(_, low):
        out = []
        for i in range(half):
            k = core * half + i
            x = split(inv[k])
            rest = 2.0 * eye(width) - dot3((ah[i], al[i]), x)
            grown = low[i] * (2.0 - low[i])
            scale = 2.0 / (1.0 + grown)
            inv[k] = scale * dot3(x, split(rest))
            out.append(scale * grown)
        return tuple(out)

    low = lax.fori_loop(0, 2, body, tuple(low))
    forward()
    low = lax.fori_loop(0, 3, body, low)
    gather()
    lax.fori_loop(0, STEPS - 7, body, low)
    for i in range(half):
        k = core * half + i
        x = inv[k]
        rest = eye(width) - jnp.dot(
            shifted[i], x, precision=lax.Precision.HIGHEST, preferred_element_type=F32
        )
        inv[k] = x + dot3(split(x), split(rest))
    at = inv.at[pl.ds(core * half, half)]
    swap = rc(at, at, sx.at[0], rx.at[0], pair)
    swap.start()
    swap.wait_recv()
    for cp in third:
        cp.wait_recv()
    swap.wait_send()
    for cp in first + third:
        cp.wait_send()
    for j in range(n_row):

        @pl.when(goal(j) != c)
        def _(j=j):
            second(j).wait_send()


def spread(n_row, n_col, panel, diag, flags):
    nodes, width = diag.shape[0], diag.shape[1]
    vm = pl.BlockSpec(memory_space=pltpu.VMEM)
    dma = pltpu.SemaphoreType.DMA
    some = (nodes // 2,) + diag.shape[1:]
    return pl.pallas_call(
        functools.partial(spread_kernel, n_row, n_col),
        out_shape=(
            jax.ShapeDtypeStruct((n_row,) + panel.shape, BF),
            jax.ShapeDtypeStruct(diag.shape, F32),
        ),
        in_specs=[vm] * 3,
        out_specs=(vm, vm),
        scratch_shapes=[
            pltpu.VMEM((n_row, nodes, panel.shape[1] // n_row, width), BF),
            pltpu.VMEM(some, F32),
            pltpu.VMEM(some, BF),
            pltpu.VMEM(some, BF),
            dma((n_row - 1,)), dma((n_row - 1,)),
            dma((n_row,)), dma((n_row,)),
            dma((n_row - 1, n_row)), dma((n_row - 1, n_row)),
            dma((1,)), dma((1,)),
        ],
        compiler_params=pltpu.CompilerParams(
            collective_id=0, has_side_effects=True, vmem_limit_bytes=48 * 2**20
        ),
        name="spread_panels_and_invert",
    )(panel, diag, flags)


def reduce_kernel(
    n_row, n_col, tile, block, normed, inv, panel_out, diag_out,
    pair_out, own, pair_in, line_out, line_in, dpart, dpair, drow, dline, piece,
    pair_s, pair_r, line_s, line_r, da_s, da_r, db_s, db_r, dc_s, dc_r,
    gc_s, gc_r, gb_s, gb_r, ga_s, ga_r,
):
    nz = n_col // 2
    nodes, width = inv.shape[0], inv.shape[1]
    r, c = lax.axis_index("row"), lax.axis_index("col")
    z, core = c // 2, lax.rem(c, 2)
    other = 1 - core
    pair = (r, z * 2 + other)

    def line(off):
        zz = lax.rem(z + off, nz)
        return zz, (r, zz * 2 + core)

    def across(off):
        rr = lax.rem(r + off, n_row)
        return rr, (rr, c)

    def rc(src, dst, s, q, dev):
        return pltpu.make_async_remote_copy(
            src_ref=src, dst_ref=dst, send_sem=s, recv_sem=q, device_id=dev, device_id_type=MESH
        )

    barrier = pltpu.get_barrier_semaphore()
    pl.semaphore_signal(barrier, inc=1, device_id=pair, device_id_type=MESH)
    for off in range(1, nz):
        pl.semaphore_signal(barrier, inc=1, device_id=line(off)[1], device_id_type=MESH)
    for off in range(1, n_row):
        pl.semaphore_signal(barrier, inc=1, device_id=across(off)[1], device_id_type=MESH)
    pl.semaphore_wait(barrier, 1 + (nz - 1) + (n_row - 1))

    count = normed.shape[0]
    order = list(range(1, nz)) + [0]
    pair_copies = {}
    line_copies = {}

    def product(index):
        at = pl.ds(pl.multiple_of(index * count, count), count)
        return jnp.dot(tile[at, :], block[...], preferred_element_type=F32)

    def to_pair(off):
        zz, _ = line(off)
        pair_out[off] = product(zz * 2 + other).astype(BF)
        pair_copies[off] = rc(pair_out.at[off], pair_in.at[off], pair_s.at[off], pair_r.at[off], pair)
        pair_copies[off].start()

    to_pair(order[0])
    for step, off in enumerate(order):
        if step + 1 < nz:
            to_pair(order[step + 1])
        zz, dev = line(off)
        own[...] = product(zz * 2 + core)
        pair_copies[off].wait_recv()
        if off == 0:
            continue
        line_out[off - 1] = (own[...] + pair_in[off].astype(F32)).astype(BF)
        line_copies[off] = rc(
            line_out.at[off - 1], line_in.at[off - 1], line_s.at[off - 1], line_r.at[off - 1], dev
        )
        line_copies[off].start()
    for off in range(1, nz):
        line_copies[off].wait_recv()

    for k in range(nodes):
        cols = pl.ds(k * width, width)
        applied = own[:, cols] + pair_in[0, :, cols].astype(F32)
        for off in range(1, nz):
            applied = applied + line_in[off - 1, :, cols].astype(F32)
        panel_out[k] = (-applied).astype(BF)
        hi, lo = split(applied)
        left = normed[:, cols]
        dims = (((0,), (0,)), ((), ()))
        dpart[k] = lax.dot_general(left, hi, dims, preferred_element_type=F32) + lax.dot_general(
            left, lo, dims, preferred_element_type=F32
        )

    half = nodes // 2
    first = core * half
    hold = pl.ds(first, half)
    copy = rc(dpart.at[pl.ds(other * half, half)], dpair, da_s.at[0], da_r.at[0], pair)
    copy.start()
    copy.wait_recv()
    dpart[hold] = dpart[hold] + dpair[...]
    copies = [copy]

    rows_b = width // n_row
    stage = []
    for off in range(1, n_row):
        rr, dev = across(off)
        cp = rc(
            dpart.at[hold, pl.ds(rr * rows_b, rows_b)],
            drow.at[off - 1], db_s.at[off - 1], db_r.at[off - 1], dev,
        )
        cp.start()
        stage.append(cp)
    start_b = pl.multiple_of(r * rows_b, rows_b)
    for cp in stage:
        cp.wait_recv()
    total = dpart[hold, pl.ds(start_b, rows_b)]
    for off in range(1, n_row):
        total = total + drow[off - 1]
    piece[...] = total
    copies += stage

    rows_c = rows_b // nz
    stage = []
    for off in range(1, nz):
        zz, dev = line(off)
        cp = rc(
            piece.at[:, pl.ds(zz * rows_c, rows_c)],
            dline.at[off - 1], dc_s.at[off - 1], dc_r.at[off - 1], dev,
        )
        cp.start()
        stage.append(cp)
    start_c = pl.multiple_of(z * rows_c, rows_c)
    for cp in stage:
        cp.wait_recv()
    total = piece[:, pl.ds(start_c, rows_c)]
    for off in range(1, nz):
        total = total + dline[off - 1]
    mine = pl.multiple_of(start_b + start_c, rows_c)
    diag_out[hold, pl.ds(mine, rows_c)] = total + inv[hold, pl.ds(mine, rows_c)]
    copies += stage

    stage = []
    for off in range(1, nz):
        _, dev = line(off)
        at = diag_out.at[hold, pl.ds(mine, rows_c)]
        cp = rc(at, at, gc_s.at[off - 1], gc_r.at[off - 1], dev)
        cp.start()
        stage.append(cp)
    for cp in stage:
        cp.wait_recv()
    copies += stage
    stage = []
    for off in range(1, n_row):
        _, dev = across(off)
        at = diag_out.at[hold, pl.ds(start_b, rows_b)]
        cp = rc(at, at, gb_s.at[off - 1], gb_r.at[off - 1], dev)
        cp.start()
        stage.append(cp)
    for cp in stage:
        cp.wait_recv()
    copies += stage
    at = diag_out.at[hold]
    cp = rc(at, at, ga_s.at[0], ga_r.at[0], pair)
    cp.start()
    cp.wait_recv()
    copies.append(cp)
    for off in order:
        pair_copies[off].wait_send()
    for off in range(1, nz):
        line_copies[off].wait_send()
    for cp in copies:
        cp.wait_send()


def reduce(n_row, n_col, tile, block, normed, inv):
    nz = n_col // 2
    nodes, width = inv.shape[0], inv.shape[1]
    rows = normed.shape[0]
    half = nodes // 2
    rows_b = width // n_row
    rows_c = rows_b // nz
    vm = pl.BlockSpec(memory_space=pltpu.VMEM)
    dma = pltpu.SemaphoreType.DMA
    return pl.pallas_call(
        functools.partial(reduce_kernel, n_row, n_col),
        out_shape=(
            jax.ShapeDtypeStruct((nodes, rows, width), BF),
            jax.ShapeDtypeStruct(inv.shape, F32),
        ),
        in_specs=[vm] * 4,
        out_specs=(vm, vm),
        scratch_shapes=[
            pltpu.VMEM((nz, rows, nodes * width), BF),
            pltpu.VMEM((rows, nodes * width), F32),
            pltpu.VMEM((nz, rows, nodes * width), BF),
            pltpu.VMEM((nz - 1, rows, nodes * width), BF),
            pltpu.VMEM((nz - 1, rows, nodes * width), BF),
            pltpu.VMEM(inv.shape, F32),
            pltpu.VMEM((half, width, width), F32),
            pltpu.VMEM((n_row - 1, half, rows_b, width), F32),
            pltpu.VMEM((nz - 1, half, rows_c, width), F32),
            pltpu.VMEM((half, rows_b, width), F32),
            dma((nz,)), dma((nz,)), dma((nz - 1,)), dma((nz - 1,)),
            dma((1,)), dma((1,)), dma((n_row - 1,)), dma((n_row - 1,)),
            dma((nz - 1,)), dma((nz - 1,)), dma((nz - 1,)), dma((nz - 1,)),
            dma((n_row - 1,)), dma((n_row - 1,)), dma((1,)), dma((1,)),
        ],
        compiler_params=pltpu.CompilerParams(
            collective_id=1, has_side_effects=True, vmem_limit_bytes=58 * 2**20
        ),
        name="sum_products_and_diagonals",
    )(tile, block, normed, inv)


def normalize(rows, inv):
    hi, lo = split(inv)
    dims = (((2,), (1,)), ((0,), (0,)))
    d = functools.partial(lax.dot_general, dimension_numbers=dims, preferred_element_type=F32)
    return (d(rows, hi) + d(rows, lo)).astype(BF)


def local(n_row, n_col, diag_blocks, pivot_flags, panels, structure, ancestor_inverse):
    nodes, rows, width = panels.shape
    masked = panels * structure.astype(BF)[:, :, None]
    column, inv = spread(n_row, n_col, masked, diag_blocks, pivot_flags[:, None, :])
    column = column.transpose(1, 0, 2, 3).reshape(nodes, n_row * rows, width)
    block = normalize(column, inv).transpose(1, 0, 2).reshape(n_row * rows, nodes * width)
    own = normalize(masked, inv).transpose(1, 0, 2).reshape(rows, nodes * width)
    return reduce(n_row, n_col, ancestor_inverse, block, own, inv)


def solution(mesh):
    in_specs = (P(), P(), P(None, ("row", "col"), None), P(None, ("row", "col")), P("row", "col"))
    out_specs = (P(None, ("row", "col"), None), P())
    body = functools.partial(local, mesh.shape["row"], mesh.shape["col"])
    return jax.shard_map(body, mesh=mesh, in_specs=in_specs, out_specs=out_specs, check_vma=False)
```
